32 devices in a mesh: dom: 32 (over z, y, x, core).
Axes of the slice: x: 2, y: 2, z: 4, core: 2. Of those that a mesh axis runs over, the one named last changes fastest.
Arguments:
- q_state: float32 [9, 56, 4096], P(None, None, 'dom'), may hold values from -6 to 6
- star_mats: float32 [3, 9, 9, 4096], P(None, None, None, 'dom'), may hold values from -3 to 3
- flux_minus: float32 [4, 9, 9, 4096], P(None, None, None, 'dom'), may hold values from -2 to 2
- flux_plus: float32 [4, 9, 9, 4096], P(None, None, None, 'dom'), may hold values from -2 to 2
- time_limit: float32 [4096], P('dom'), may hold values from 0.25 to 3.6
- deriv_mats: float32 [3, 56, 56], replicated, may hold values from -0.75 to 0.75
- volume_mats: float32 [3, 56, 56], replicated, may hold values from -0.75 to 0.75
- face_proj: float32 [4, 21, 56], replicated, may hold values from -0.75 to 0.75
- face_lift: float32 [4, 56, 21], replicated, may hold values from -1.25 to 1.25
- face_link: int32 [4, 4096], P(None, 'dom'), may hold values from -1 to 895, as said below
- face_orient: int32 [4, 4096], P(None, 'dom'), may hold values from 0 to 2
- send_face: int32 [6, 2048], P(None, 'dom'), may hold values from -1 to 511, as said below
Outputs:
- q_new: float32 [9, 56, 4096], P(None, None, 'dom')
The draws below stay inside these ranges and needn't reach their ends.
Inputs may be any that keep to these rules, and one draw needn't show every extreme that they name: For face f of element e of a partition, v = face_link[f, d * 128 + e]: -1 is an absorbing boundary; v < 512 names face v // 128 of element v % 128 of the same partition; otherwise v = 512 + k * 64 + s names slot s of received block k, and s is below the number of faces that the partition at offset o_k sends it. No block holds more than 64 faces, and some blocks are full. `send_face`: row k of a partition's 64 columns lists the faces f * 128 + e that it sends to the partition at offset - o_k, then -1 in the unused slots; their number equals what that partition reads from the block; no face stands twice on a partition.
All inputs are finite; a program needn't handle non-finite values.
Results may differ from the reference program's by a relative error of at most 0.0003.
Values sent between devices are 32-bit elements; how exact they have to be, the bound alone decides.
A program may use at most 128 MiB of HBM per device.

```python
import math
import jax
import jax.numpy as jnp
import numpy as np
from jax import lax

NQ = 9
NB = 56
NF = 21
ORDER = 6
REACH = 3
SCAP = 64
FINE_DEV = 64
NOFF = 6
E_DEV = 128
ELEMS = 4096
N_DOM = 32


def block_offsets():
    return jnp.array([position - REACH if position < REACH else position - REACH + 1 for position in range(NOFF)], dtype=jnp.int32)


def mesh_links(key):
    base_key = jax.random.fold_in(key, 7103)
    device_ids = jnp.arange(N_DOM, dtype=jnp.int32)
    offsets = block_offsets()
    source = device_ids[:, None] + offsets[None, :]
    present = (source >= 0) & (source < N_DOM)
    raw_counts = jax.random.randint(jax.random.fold_in(base_key, 1), (N_DOM, NOFF), SCAP // 4, SCAP + 1, dtype=jnp.int32)
    filled = (device_ids[:, None] + jnp.arange(NOFF, dtype=jnp.int32)[None, :]) % 3 == 0
    counts = jnp.where(present, jnp.where(filled, SCAP, raw_counts), 0).astype(jnp.int32)
    face_total = 4 * E_DEV
    positions = jnp.arange(face_total, dtype=jnp.int32)

    def receiver(device_key, row_counts):
        perm_key, local_key = jax.random.split(device_key)
        placing = jax.random.permutation(perm_key, face_total).astype(jnp.int32)
        block_ends = jnp.cumsum(row_counts).astype(jnp.int32)
        block_starts = block_ends - row_counts
        block_index = jnp.minimum(jnp.sum((positions[:, None] >= block_ends[None, :]).astype(jnp.int32), axis=1), NOFF - 1)
        remote = face_total + block_index * SCAP + positions - block_starts[block_index]
        local_link = jax.random.randint(local_key, (face_total,), 0, face_total, dtype=jnp.int32)
        remote_total = block_ends[NOFF - 1]
        link_value = jnp.where(positions < remote_total, remote, jnp.where(positions < remote_total + E_DEV // 4, -1, local_link))
        inverse = jnp.argsort(placing)
        return link_value[inverse].reshape(4, E_DEV).astype(jnp.int32)
    receive_keys = jax.vmap(lambda number: jax.random.fold_in(jax.random.fold_in(base_key, 2), number))(device_ids)
    link_table = jax.vmap(receiver)(receive_keys, counts)
    target = device_ids[:, None] - offsets[None, :]
    target_valid = (target >= 0) & (target < N_DOM)
    send_counts = jnp.where(target_valid, counts[jnp.clip(target, 0, N_DOM - 1), jnp.arange(NOFF, dtype=jnp.int32)[None, :]], 0)

    def sender(device_key, row_counts):
        chosen = jax.random.permutation(device_key, face_total).astype(jnp.int32)[:NOFF * SCAP].reshape(NOFF, SCAP)
        slot_index = jnp.arange(SCAP, dtype=jnp.int32)[None, :]
        return jnp.where(slot_index < row_counts[:, None], chosen, -1).astype(jnp.int32)
    send_keys = jax.vmap(lambda number: jax.random.fold_in(jax.random.fold_in(base_key, 3), number))(device_ids)
    send_table = jax.vmap(sender)(send_keys, send_counts)
    links_out = jnp.transpose(link_table, (1, 0, 2)).reshape(4, N_DOM * E_DEV)
    sends_out = jnp.transpose(send_table, (1, 0, 2)).reshape(NOFF, N_DOM * SCAP)
    return (links_out, sends_out)


def draw_face_link(key, part):
    return mesh_links(key)[0]


def draw_send_face(key, part):
    return mesh_links(key)[1]


def draw_time_limit(key, part):
    device_key, element_key = jax.random.split(key)
    device_pos = jnp.arange(N_DOM, dtype=jnp.float32)[:, None] / max(N_DOM - 1, 1)
    cluster = jnp.where(jnp.arange(E_DEV)[None, :] < FINE_DEV, 1.0, 2.0)
    device_factor = jnp.exp(math.log(2.0) * jax.random.uniform(device_key, (N_DOM, 1), jnp.float32))
    element_factor = 1.0 + 0.2 * jax.random.uniform(element_key, (N_DOM, E_DEV), jnp.float32)
    limits = 0.25 * cluster * (1.0 + 2.0 * device_pos) * device_factor * element_factor
    return limits.reshape(N_DOM * E_DEV).astype(jnp.float32)


def set_ends(entries, own_key, least, largest):
    spot = [jax.random.randint(jax.random.fold_in(own_key, axis), (), 0, length) for axis, length in enumerate(entries.shape)]
    longest = entries.shape.index(max(entries.shape))
    beside = spot[:longest] + [(spot[longest] + 1) % entries.shape[longest]] + spot[longest + 1:]
    return entries.at[tuple(spot)].set(least).at[tuple(beside)].set(largest)


def shard_levels(own_key, shape, cuts, low, largest):
    factor_of, own = 1.0, jax.random.fold_in(own_key, 6)
    for dim, shards_of in cuts:
        draws = jnp.exp(jax.random.uniform(jax.random.fold_in(own, dim), (shards_of,), jnp.float32, low / len(cuts), largest / len(cuts)))
        factor_of = factor_of * jnp.repeat(draws, shape[dim] // shards_of).reshape([-1 if axis == dim else 1 for axis in range(len(shape))])
    return factor_of


def normal_values(key, extent, width, reach, shards=(), kind=jnp.bfloat16):
    drawn = width * jax.random.normal(key, extent, jnp.float32)
    if shards:
        drawn = drawn * shard_levels(key, extent, shards, -0.22, 0.18)
    return jnp.clip(drawn, -reach, reach).astype(kind)


def setup_inputs(seed: int = 0) -> dict:
    arg_keys = jax.random.split(jax.random.key(seed), 13)
    q_state = normal_values(arg_keys[0], (NQ, NB, ELEMS), 1.0, 6.0, ((2, 32),), jnp.float32)
    star_mats = normal_values(arg_keys[1], (3, NQ, NQ, ELEMS), 0.6, 3.0, ((3, 32),), jnp.float32)
    flux_minus = normal_values(arg_keys[2], (4, NQ, NQ, ELEMS), NQ ** -0.5, 2.0, ((3, 32),), jnp.float32)
    flux_plus = normal_values(arg_keys[3], (4, NQ, NQ, ELEMS), NQ ** -0.5, 2.0, ((3, 32),), jnp.float32)
    time_limit = draw_time_limit(jax.random.fold_in(arg_keys[12], 71), 0)
    deriv_mats = normal_values(arg_keys[5], (3, NB, NB), NB ** -0.5, 0.75, (), jnp.float32)
    volume_mats = normal_values(arg_keys[6], (3, NB, NB), NB ** -0.5, 0.75, (), jnp.float32)
    face_proj = normal_values(arg_keys[7], (4, NF, NB), NB ** -0.5, 0.75, (), jnp.float32)
    face_lift = normal_values(arg_keys[8], (4, NB, NF), NF ** -0.5, 1.25, (), jnp.float32)
    face_link = draw_face_link(jax.random.fold_in(arg_keys[12], 71), 0)
    face_orient = set_ends(jax.random.randint(arg_keys[10], (4, ELEMS), 0, 3), jax.random.fold_in(arg_keys[10], 1), 0, 2).astype(jnp.int32)
    send_face = draw_send_face(jax.random.fold_in(arg_keys[12], 71), 0)
    return {"q_state": q_state, "star_mats": star_mats, "flux_minus": flux_minus, "flux_plus": flux_plus, "time_limit": time_limit, "deriv_mats": deriv_mats, "volume_mats": volume_mats, "face_proj": face_proj, "face_lift": face_lift, "face_link": face_link, "face_orient": face_orient, "send_face": send_face}


HIGH = lax.Precision.HIGHEST
STEP_RATIO = 2.0


def rotation_table(node_count):
    degree = 0
    while (degree + 1) * (degree + 2) // 2 < node_count:
        degree += 1
    node_pairs = [(across, upward) for across in range(degree + 1) for upward in range(degree + 1 - across)]
    lookup = {}
    for number, node_pair in enumerate(node_pairs):
        lookup[node_pair] = number
    tables = []
    for rotations in range(3):
        new_order = []
        for node_pair in node_pairs:
            moved_pair = (node_pair[1], node_pair[0])
            for repeat in range(rotations):
                moved_pair = (moved_pair[1], degree - moved_pair[0] - moved_pair[1])
            new_order.append(lookup[moved_pair])
        tables.append(new_order)
    return np.array(tables, dtype=np.int32)


def taylor_series(coeffs, star_part, deriv_mats):
    series = [coeffs]
    current = coeffs
    for term_index in range(ORDER - 1):
        derived = jnp.einsum('dbc,qce->dbqe', deriv_mats, current, precision=HIGH)
        current = -jnp.sum(star_part[:, :, :, None, :] * jnp.swapaxes(derived, 1, 2)[:, None, :, :, :], axis=(0, 2))
        series.append(current)
    return series


def integrate(series, start_time, end_time):
    summed = (end_time - start_time) * series[0]
    for term_index in range(1, len(series)):
        weight = (end_time ** (term_index + 1) - start_time ** (term_index + 1)) / math.factorial(term_index + 1)
        summed = summed + weight * series[term_index]
    return summed


def face_values(integral, face_proj):
    projected = jnp.einsum('fnb,qbe->qnfe', face_proj, integral, precision=HIGH)
    return projected.reshape(projected.shape[0], projected.shape[1], -1)


def neighbour_faces(face_pool, face_links, orients, rotation):
    face_count = face_links.shape[0] * face_links.shape[1]
    padded = jnp.concatenate([face_pool, jnp.zeros((face_pool.shape[0], face_pool.shape[1], 1), face_pool.dtype)], axis=2)
    indices = jnp.where(face_links < 0, face_pool.shape[2], face_links).reshape(face_count)
    picked = jnp.take(padded, indices, axis=2)
    orient_codes = orients.reshape(face_count)
    turned = jnp.where(orient_codes == 0, picked[:, rotation[0], :],
                       jnp.where(orient_codes == 1, picked[:, rotation[1], :], picked[:, rotation[2], :]))
    return turned.reshape(face_pool.shape[0], face_pool.shape[1], face_links.shape[0], face_links.shape[1])


def face_flux(solver_part, face_data):
    moved = jnp.transpose(face_data, (2, 0, 1, 3))
    return jnp.sum(solver_part[:, :, :, None, :] * moved[:, None, :, :, :], axis=2)


def advance(coeffs, integral, own_faces, neighbour, star_part, volume_mats, face_lift, minus_part, plus_part):
    starred = jnp.sum(star_part[:, :, :, None, :] * integral[None, None, :, :, :], axis=2)
    gained = jnp.einsum('dbc,dpce->pbe', volume_mats, starred, precision=HIGH)
    across = face_flux(minus_part, own_faces) + face_flux(plus_part, neighbour)
    lifted = jnp.einsum('fbn,fpne->pbe', face_lift, across, precision=HIGH)
    return coeffs + gained - lifted


def pack_blocks(faces_flat, sends):
    padded = jnp.concatenate([faces_flat, jnp.zeros((faces_flat.shape[0], faces_flat.shape[1], 1), faces_flat.dtype)], axis=2)
    indices = jnp.where(sends < 0, faces_flat.shape[2], sends).reshape(sends.shape[0] * sends.shape[1])
    picked = jnp.take(padded, indices, axis=2)
    return picked.reshape(faces_flat.shape[0], faces_flat.shape[1], sends.shape[0], sends.shape[1])


def route(send_blocks):
    device_ids = jnp.arange(N_DOM)
    gathered = []
    for position in range(NOFF):
        offset = position - REACH if position < REACH else position - REACH + 1
        rolled = jnp.roll(send_blocks[:, :, :, position, :], -offset, axis=0)
        present = (device_ids + offset >= 0) & (device_ids + offset < N_DOM)
        gathered.append(jnp.where(present[:, None, None, None], rolled, 0.0))
    stacked = jnp.stack(gathered, axis=3)
    return stacked.reshape(N_DOM, NQ, NF, NOFF * SCAP)


def reference(q_state, star_mats, flux_minus, flux_plus, time_limit, deriv_mats, volume_mats, face_proj, face_lift, face_link, face_orient, send_face):
    rotation = rotation_table(NF)

    def by_device(array):
        shaped = array.reshape(array.shape[:-1] + (N_DOM, E_DEV))
        return jnp.moveaxis(shaped, -2, 0)

    coeff_all = by_device(q_state)
    star_all = by_device(star_mats)
    minus_all = by_device(flux_minus)
    plus_all = by_device(flux_plus)
    link_all = by_device(face_link)
    orient_all = by_device(face_orient)
    send_all = jnp.moveaxis(send_face.reshape(NOFF, N_DOM, SCAP), 1, 0)
    local_index = jnp.arange(ELEMS) % E_DEV
    allowed = jnp.where(local_index < FINE_DEV, time_limit, time_limit / STEP_RATIO)
    step_fine = jnp.min(allowed)
    step_coarse = STEP_RATIO * step_fine

    def device_work(device_item, depth):
        coeffs, star_dev, minus_dev, plus_dev, links, orients, sends, received_one, received_two = device_item
        fine_star = star_dev[..., :FINE_DEV]
        coarse_star = star_dev[..., FINE_DEV:]
        fine_series = taylor_series(coeffs[:, :, :FINE_DEV], fine_star, deriv_mats)
        coarse_series = taylor_series(coeffs[:, :, FINE_DEV:], coarse_star, deriv_mats)
        fine_one = integrate(fine_series, 0.0, step_fine)
        coarse_one = integrate(coarse_series, 0.0, step_fine)
        coarse_two = integrate(coarse_series, step_fine, step_coarse)
        faces_one = face_values(jnp.concatenate([fine_one, coarse_one], axis=2), face_proj)
        if depth == 1:
            return pack_blocks(faces_one, sends)
        fine_links = links[:, :FINE_DEV]
        fine_orients = orients[:, :FINE_DEV]
        fine_minus = minus_dev[..., :FINE_DEV]
        fine_plus = plus_dev[..., :FINE_DEV]
        shaped_one = faces_one.reshape(NQ, NF, 4, E_DEV)
        pool_one = jnp.concatenate([faces_one, received_one], axis=2)
        fine_mid = advance(coeffs[:, :, :FINE_DEV], fine_one, shaped_one[..., :FINE_DEV],
                           neighbour_faces(pool_one, fine_links, fine_orients, rotation),
                           fine_star, volume_mats, face_lift, fine_minus, fine_plus)
        fine_two = integrate(taylor_series(fine_mid, fine_star, deriv_mats), 0.0, step_fine)
        faces_two = face_values(jnp.concatenate([fine_two, coarse_two], axis=2), face_proj)
        if depth == 2:
            return pack_blocks(faces_two, sends)
        shaped_two = faces_two.reshape(NQ, NF, 4, E_DEV)
        pool_two = jnp.concatenate([faces_two, received_two], axis=2)
        fine_end = advance(fine_mid, fine_two, shaped_two[..., :FINE_DEV],
                           neighbour_faces(pool_two, fine_links, fine_orients, rotation),
                           fine_star, volume_mats, face_lift, fine_minus, fine_plus)
        pool_both = jnp.concatenate([faces_one + faces_two, received_one + received_two], axis=2)
        coarse_end = advance(coeffs[:, :, FINE_DEV:], coarse_one + coarse_two, (shaped_one + shaped_two)[..., FINE_DEV:],
                             neighbour_faces(pool_both, links[:, FINE_DEV:], orients[:, FINE_DEV:], rotation),
                             coarse_star, volume_mats, face_lift, minus_dev[..., FINE_DEV:], plus_dev[..., FINE_DEV:])
        return jnp.concatenate([fine_end, coarse_end], axis=2)

    blank = jnp.zeros((N_DOM, NQ, NF, NOFF * SCAP), jnp.float32)
    common = (coeff_all, star_all, minus_all, plus_all, link_all, orient_all, send_all)
    sends_one = lax.map(lambda device_item: device_work(device_item, 1), common + (blank, blank))
    received_one = route(sends_one)
    sends_two = lax.map(lambda device_item: device_work(device_item, 2), common + (received_one, blank))
    received_two = route(sends_two)
    updated = lax.map(lambda device_item: device_work(device_item, 3), common + (received_one, received_two))
    return jnp.moveaxis(updated, 0, -2).reshape(NQ, NB, ELEMS)
```

```python
import functools
import math

import jax
import jax.numpy as jnp
import numpy as np
from jax import lax
from jax.experimental import pallas as pl
from jax.experimental.pallas import tpu as pltpu
from jax.sharding import PartitionSpec as P

ORDER = 6
REACH = 3
FINE_DEV = 64
NODE_PAD = 24
F32 = jnp.float32
BF16 = jnp.bfloat16
MESH = pl.DeviceIdType.MESH


def rotation_table(node_count):
    degree = 0
    while (degree + 1) * (degree + 2) // 2 < node_count:
        degree += 1
    node_pairs = [
        (across, upward) for across in range(degree + 1) for upward in range(degree + 1 - across)
    ]
    lookup = {pair: number for number, pair in enumerate(node_pairs)}
    tables = []
    for rotations in range(3):
        new_order = []
        for node_pair in node_pairs:
            moved_pair = (node_pair[1], node_pair[0])
            for repeat in range(rotations):
                moved_pair = (moved_pair[1], degree - moved_pair[0] - moved_pair[1])
            new_order.append(lookup[moved_pair])
        tables.append(new_order)
    return np.array(tables, dtype=np.int32)


def round_up(value, step):
    return (value + step - 1) // step * step


def radices(count):
    out = []
    while count > 1:
        radix = max([r for r in range(2, 9) if count % r == 0], default=count)
        out.append(radix)
        count //= radix
    return out


def offset_of(position):
    return position - REACH if position < REACH else position - REACH + 1


def split(value):
    high = value.astype(BF16)
    low = (value - high.astype(F32)).astype(BF16)
    return high, low


def dot(a, b):
    return jnp.dot(a, b, preferred_element_type=F32)


def kernel(
    count,
    nq,
    nb,
    nf,
    q_ref,
    star_ref,
    minus_ref,
    plus_ref,
    limit_ref,
    deriv_ref,
    volume_ref,
    proj_ref,
    lift_ref,
    link_ref,
    orient_ref,
    send_ref,
    compact_ref,
    rotate_ref,
    out_ref,
    a_der,
    a_vol,
    a_proj,
    a_lift,
    s_local,
    s_remote,
    t_send,
    series,
    b_mat,
    r_mat,
    vol,
    own,
    ic_two,
    io,
    faces,
    pool,
    picked,
    turned,
    across,
    b_lift,
    base,
    min_out,
    min_in,
    send_buf,
    recv_buf,
    min_send_sem,
    min_recv_sem,
    send_sem,
    recv_sem,
):
    elems = q_ref.shape[2]
    lanes = lax.broadcasted_iota(jnp.int32, (1, elems), 1)
    is_fine = lanes < FINE_DEV
    me = lax.axis_index("dom")
    bp = b_mat.shape[0] // 3
    rows_c = pool.shape[0] // 2
    half = rows_c // 2
    digits = radices(count)

    def peer_of(number, step):
        stride = math.prod(digits[:number])
        radix = digits[number]
        digit = lax.rem(me // stride, radix)
        return me + (lax.rem(digit + step, radix) - digit) * stride

    barrier = pltpu.get_barrier_semaphore()
    expected = 0
    for number, radix in enumerate(digits):
        for step in range(1, radix):
            pl.semaphore_signal(
                barrier, inc=1, device_id=(peer_of(number, step),), device_id_type=MESH
            )
            expected += 1
    for position in range(2 * REACH):
        target = me - offset_of(position)

        @pl.when((target >= 0) & (target < count))
        def _():
            pl.semaphore_signal(barrier, inc=1, device_id=(target,), device_id_type=MESH)

    least = jnp.where(is_fine, limit_ref[...], limit_ref[...] * 0.5)
    least = jnp.broadcast_to(jnp.min(least, axis=1, keepdims=True), (8, elems))

    below = jnp.minimum(me, REACH)
    above = jnp.minimum(count - 1 - me, REACH)
    pl.semaphore_wait(barrier, expected + below + above)

    def min_copy(number, step):
        return pltpu.make_async_remote_copy(
            src_ref=min_out.at[number],
            dst_ref=min_in.at[number, step - 1],
            send_sem=min_send_sem.at[number, step - 1],
            recv_sem=min_recv_sem.at[number, step - 1],
            device_id=(peer_of(number, step),),
            device_id_type=MESH,
        )

    def min_start(number, value):
        min_out[number] = value
        for step in range(1, digits[number]):
            min_copy(number, step).start()

    def min_finish(number, value):
        for step in range(1, digits[number]):
            min_copy(number, step).wait_recv()
        for step in range(1, digits[number]):
            value = jnp.minimum(value, min_in[number, step - 1])
        return value

    if digits:
        min_start(0, least)

    def wide(x, width):
        high = x.astype(BF16).astype(F32)
        low = x - high
        if width > x.shape[1]:
            z = jnp.zeros((x.shape[0], width - x.shape[1]), F32)
            parts = [high, z, high, z, low, z]
        else:
            parts = [high, high, low]
        return jnp.concatenate(parts, axis=1)

    for d in range(3):
        r_mat[d * nb : (d + 1) * nb, 0 : 3 * bp] = wide(deriv_ref[d], bp)
    a_der[...] = r_mat[0 : 3 * nb, 0 : 3 * bp].astype(BF16)
    for d in range(3):
        r_mat[d * nb : (d + 1) * nb, 0 : 3 * bp] = wide(volume_ref[d], bp)
    a_vol[...] = r_mat[0 : 3 * nb, 0 : 3 * bp].astype(BF16)
    r_mat[0 : 4 * NODE_PAD, 0 : 3 * bp] = jnp.zeros((4 * NODE_PAD, 3 * bp), F32)
    for f in range(4):
        r_mat[f * NODE_PAD : f * NODE_PAD + nf, 0 : 3 * bp] = wide(proj_ref[:, f, :], bp)
    a_proj[...] = r_mat[0 : 4 * NODE_PAD, 0 : 3 * bp].astype(BF16)
    r_mat[0 : 4 * NODE_PAD, 0 : 128] = jnp.zeros((4 * NODE_PAD, 128), F32)
    for f in range(4):
        r_mat[f * NODE_PAD : f * NODE_PAD + nf, 0:nb] = lift_ref[:, f, :]
    turned_lift = jnp.transpose(r_mat[0 : 4 * NODE_PAD, 0:128])[0:nb]
    a_lift[...] = wide(turned_lift, 4 * NODE_PAD).astype(BF16)

    def fill(target_q, x):
        high, low = split(jnp.concatenate([x, jnp.zeros((bp - nb, elems), F32)], axis=0))
        b_mat[0:bp, target_q * elems : (target_q + 1) * elems] = high
        b_mat[bp : 2 * bp, target_q * elems : (target_q + 1) * elems] = low
        b_mat[2 * bp : 3 * bp, target_q * elems : (target_q + 1) * elems] = high

    def starred(a_ref, store):
        r_mat[...] = dot(a_ref[...], b_mat[...])

        def group(g, carry):
            sums = [None] * 3
            for d in range(3):
                for q in range(nq):
                    block = r_mat[d * nb : (d + 1) * nb, q * elems : (q + 1) * elems]
                    for i in range(3):
                        row = star_ref[g * 3 + i, q, d : d + 1, :]
                        term = row * block
                        sums[i] = term if sums[i] is None else sums[i] + term
            for i in range(3):
                store(g * 3 + i, sums[i])
            return carry

        lax.fori_loop(0, nq // 3, group, 0)

    def taylor():
        def step(k, carry):
            for q in range(nq):
                fill(q, series[k, q])

            def keep(p, value):
                series[k + 1, p] = -value

            starred(a_der, keep)
            return carry

        lax.fori_loop(0, ORDER - 1, step, 0)

    for q in range(nq):
        series[0, q] = q_ref[q]

    if digits:
        least = min_finish(0, least)
        if len(digits) > 1:
            min_start(1, least)

    taylor()

    numbers = lax.broadcasted_iota(jnp.int32, (128, elems), 0)
    own_faces = s_local.shape[0]
    for f in range(4):
        link = link_ref[f : f + 1, :]
        for v in range(0, own_faces, 128):
            s_local[v : v + 128, f * elems : (f + 1) * elems] = jnp.where(
                numbers + v == link, 1.0, 0.0
            ).astype(BF16)
        for v in range(0, s_remote.shape[0], 128):
            s_remote[v : v + 128, f * elems : (f + 1) * elems] = jnp.where(
                numbers + (v + own_faces) == link, 1.0, 0.0
            ).astype(BF16)
    for g in range(REACH):
        sends = jnp.concatenate([send_ref[2 * g : 2 * g + 1, :], send_ref[2 * g + 1 : 2 * g + 2, :]], axis=1)
        for v in range(0, own_faces, 128):
            t_send[v : v + 128, g * elems : (g + 1) * elems] = jnp.where(
                numbers + v == sends, 1.0, 0.0
            ).astype(BF16)
    faces[...] = jnp.zeros(faces.shape, F32)
    for stage in range(2):
        for position in range(2 * REACH):
            source = me + offset_of(position)

            @pl.when((source < 0) | (source >= count))
            def _():
                recv_buf[stage, position] = jnp.zeros(recv_buf.shape[2:], F32)

    for number in range(1, len(digits)):
        least = min_finish(number, least)
        if number + 1 < len(digits):
            min_start(number + 1, least)
    step_fine = least[0:1, :]

    weights = []
    weights_two = []
    power = step_fine
    for k in range(ORDER):
        weights.append(power * (1.0 / math.factorial(k + 1)))
        weights_two.append(weights[-1] * float(2 ** (k + 1) - 1))
        power = power * step_fine

    def block_copy(stage, position):
        return pltpu.make_async_remote_copy(
            src_ref=send_buf.at[stage, position],
            dst_ref=recv_buf.at[stage, position],
            send_sem=send_sem.at[stage, position],
            recv_sem=recv_sem.at[stage, position],
            device_id=(me - offset_of(position),),
            device_id_type=MESH,
        )

    def flux(solver_ref, data_ref, first):
        def face(f, carry):
            sums = [None] * nq
            for q in range(nq):
                block = data_ref[f, q * NODE_PAD : (q + 1) * NODE_PAD, :]
                for p in range(nq):
                    term = solver_ref[p, q, pl.ds(f, 1), :] * block
                    sums[p] = term if sums[p] is None else sums[p] + term
            spot = pl.ds(pl.multiple_of(f * NODE_PAD, 8), NODE_PAD)
            for p in range(nq):
                if first:
                    across[p, spot, :] = sums[p]
                else:
                    across[p, spot, :] = across[p, spot, :] + sums[p]
            return carry

        lax.fori_loop(0, 4, face, 0)

    def stage_work(stage):
        projected = dot(a_proj[...], b_mat[...])
        for f in range(4):
            for q in range(nq):
                faces[f, q * NODE_PAD : (q + 1) * NODE_PAD, :] = projected[
                    f * NODE_PAD : (f + 1) * NODE_PAD, q * elems : (q + 1) * elems
                ]
        for f in range(4):
            high, low = split(faces[f])
            pool[0:rows_c, f * elems : (f + 1) * elems] = dot(compact_ref[...], high).astype(BF16)
            pool[rows_c : 2 * rows_c, f * elems : (f + 1) * elems] = dot(
                compact_ref[...], low
            ).astype(BF16)
        for g in range(REACH):
            packed = dot(pool[...], t_send[:, g * elems : (g + 1) * elems])
            packed = packed[0:rows_c] + packed[rows_c : 2 * rows_c]
            upper, lower = packed[0:half], packed[half:rows_c]
            send_buf[stage, 2 * g] = jnp.where(is_fine, upper, pltpu.roll(lower, FINE_DEV, 1))
            send_buf[stage, 2 * g + 1] = jnp.where(is_fine, pltpu.roll(upper, FINE_DEV, 1), lower)
            for position in (2 * g, 2 * g + 1):
                target = me - offset_of(position)

                @pl.when((target >= 0) & (target < count))
                def _():
                    block_copy(stage, position).start()

        picked[...] = dot(pool[...], s_local[...])
        if stage == 0:
            own[...] = faces[...]
        else:
            for f in range(4):
                own[f] = jnp.where(is_fine, faces[f], faces[f] + own[f])
            for q in range(nq):
                fill(q, io[q])

        def keep(p, value):
            vol[p] = value

        starred(a_vol, keep)
        flux(minus_ref, own, True)

        for position in range(2 * REACH):
            source = me + offset_of(position)

            @pl.when((source >= 0) & (source < count))
            def _():
                block_copy(stage, position).wait_recv()

        for g in range(REACH):
            first, second = recv_buf[stage, 2 * g], recv_buf[stage, 2 * g + 1]
            upper = jnp.where(is_fine, first, pltpu.roll(second, FINE_DEV, 1))
            lower = jnp.where(is_fine, pltpu.roll(first, FINE_DEV, 1), second)
            high, low = split(jnp.concatenate([upper, lower], axis=0))
            pool[0:rows_c, g * elems : (g + 1) * elems] = high
            pool[rows_c : 2 * rows_c, g * elems : (g + 1) * elems] = low
        remote = s_remote.shape[0]
        total = (picked[...] + dot(pool[:, 0:remote], s_remote[...])).astype(BF16)
        rows_n = rotate_ref.shape[0] // 3
        for f in range(4):
            three = dot(rotate_ref[...], total[:, f * elems : (f + 1) * elems])
            code = orient_ref[f : f + 1, :]
            new = jnp.where(
                code == 0,
                three[0:rows_n],
                jnp.where(code == 1, three[rows_n : 2 * rows_n], three[2 * rows_n :]),
            )
            if stage == 0:
                turned[f] = new
            else:
                turned[f] = jnp.where(is_fine, new, new + turned[f])
        flux(plus_ref, turned, False)
        for p in range(nq):
            high, low = split(across[p])
            rows = 4 * NODE_PAD
            b_lift[0:rows, p * elems : (p + 1) * elems] = high
            b_lift[rows : 2 * rows, p * elems : (p + 1) * elems] = low
            b_lift[2 * rows : 3 * rows, p * elems : (p + 1) * elems] = high
        return dot(a_lift[...], b_lift[...])

    def weighted(q, table):
        total = table[0] * series[0, q]
        for k in range(1, ORDER):
            total = total + table[k] * series[k, q]
        return total

    for q in range(nq):
        one = weighted(q, weights)
        two = weighted(q, weights_two)
        fill(q, one)
        ic_two[q] = jnp.where(is_fine, 0.0, two)
        io[q] = jnp.where(is_fine, 0.0, one + two)
    lifted = stage_work(0)
    for p in range(nq):
        mid = q_ref[p] + vol[p] - lifted[:, p * elems : (p + 1) * elems]
        base[p] = jnp.where(is_fine, mid, q_ref[p])
        series[0, p] = jnp.where(is_fine, mid, 0.0)
    taylor()
    for q in range(nq):
        one = weighted(q, weights)
        fill(q, one + ic_two[q])
        io[q] = one + io[q]
    lifted = stage_work(1)
    for p in range(nq):
        out_ref[p] = base[p] + vol[p] - lifted[:, p * elems : (p + 1) * elems]

    for number, radix in enumerate(digits):
        for step in range(1, radix):
            min_copy(number, step).wait_send()
    for stage in range(2):
        for position in range(2 * REACH):
            target = me - offset_of(position)

            @pl.when((target >= 0) & (target < count))
            def _():
                block_copy(stage, position).wait_send()


def local(count, *args):
    q_state, face_proj, send_face = args[0], args[7], args[11]
    nq, nb, elems = q_state.shape
    nf = face_proj.shape[1]
    slots = send_face.shape[0] * send_face.shape[1]
    bp = round_up(nb, 16)
    rows_n = round_up(nq * NODE_PAD, 16)
    rows_c = round_up(nq * nf, 32)
    compact = np.zeros((rows_c, rows_n), np.float32)
    rotate = np.zeros((3 * rows_n, 2 * rows_c), np.float32)
    table = rotation_table(nf)
    for q in range(nq):
        for n in range(nf):
            compact[q * nf + n, q * NODE_PAD + n] = 1
            for h in range(3):
                rotate[h * rows_n + q * NODE_PAD + n, q * nf + table[h, n]] = 1
                rotate[h * rows_n + q * NODE_PAD + n, rows_c + q * nf + table[h, n]] = 1
    args = list(args)
    for number in (1, 2, 3):
        args[number] = jnp.transpose(args[number], (1, 2, 0, 3))
    args[4] = args[4].reshape(1, elems)
    args[7] = jnp.transpose(args[7], (1, 0, 2))
    args[8] = jnp.transpose(args[8], (2, 0, 1))
    args += [jnp.asarray(compact, BF16), jnp.asarray(rotate, BF16)]
    rounds = max(len(radices(count)), 1)
    widest = max([r - 1 for r in radices(count)] + [1])
    vm = pltpu.VMEM
    scratch = [
        vm((3 * nb, 3 * bp), BF16),
        vm((3 * nb, 3 * bp), BF16),
        vm((4 * NODE_PAD, 3 * bp), BF16),
        vm((nb, 12 * NODE_PAD), BF16),
        vm((4 * elems, 4 * elems), BF16),
        vm((slots, 4 * elems), BF16),
        vm((4 * elems, slots), BF16),
        vm((ORDER, nq, nb, elems), F32),
        vm((3 * bp, nq * elems), BF16),
        vm((3 * nb, nq * elems), F32),
        vm((nq, nb, elems), F32),
        vm((4, rows_n, elems), F32),
        vm((nq, nb, elems), F32),
        vm((nq, nb, elems), F32),
        vm((4, rows_n, elems), F32),
        vm((2 * rows_c, 4 * elems), BF16),
        vm((2 * rows_c, 4 * elems), F32),
        vm((4, rows_n, elems), F32),
        vm((nq, 4 * NODE_PAD, elems), F32),
        vm((12 * NODE_PAD, nq * elems), BF16),
        vm((nq, nb, elems), F32),
        vm((rounds, 8, elems), F32),
        vm((rounds, widest, 8, elems), F32),
        vm((2, 2 * REACH, rows_c // 2, elems), F32),
        vm((2, 2 * REACH, rows_c // 2, elems), F32),
        pltpu.SemaphoreType.DMA((rounds, widest)),
        pltpu.SemaphoreType.DMA((rounds, widest)),
        pltpu.SemaphoreType.DMA((2, 2 * REACH)),
        pltpu.SemaphoreType.DMA((2, 2 * REACH)),
    ]
    return pl.pallas_call(
        functools.partial(kernel, count, nq, nb, nf),
        out_shape=jax.ShapeDtypeStruct(q_state.shape, F32),
        in_specs=[pl.BlockSpec(memory_space=pltpu.VMEM)] * len(args),
        out_specs=pl.BlockSpec(memory_space=pltpu.VMEM),
        scratch_shapes=scratch,
        compiler_params=pltpu.CompilerParams(
            collective_id=0, has_side_effects=True, vmem_limit_bytes=40 * 1024 * 1024
        ),
    )(*args)


def solution(mesh):
    placed = (
        P(None, None, "dom"),
        P(None, None, None, "dom"),
        P(None, None, None, "dom"),
        P(None, None, None, "dom"),
        P("dom"),
        P(),
        P(),
        P(),
        P(),
        P(None, "dom"),
        P(None, "dom"),
        P(None, "dom"),
    )
    count = mesh.shape["dom"]
    return jax.shard_map(
        functools.partial(local, count),
        mesh=mesh,
        in_specs=placed,
        out_specs=P(None, None, "dom"),
        check_vma=False,
    )
```

```python
import functools
import math

import jax
import jax.numpy as jnp
import numpy as np
from jax import lax
from jax.experimental import pallas as pl
from jax.experimental.pallas import tpu as pltpu
from jax.sharding import PartitionSpec as P

ORDER = 6
REACH = 3
FINE_DEV = 64
NODE_PAD = 24
F32 = jnp.float32
BF16 = jnp.bfloat16
MESH = pl.DeviceIdType.MESH
OPERANDS = 14
SEND_ORDER = (0, 5, 1, 4, 2, 3)
GROUP_SPOT = (0, 2, 1)


def rotation_table(node_count):
    degree = 0
    while (degree + 1) * (degree + 2) // 2 < node_count:
        degree += 1
    node_pairs = [
        (across, upward) for across in range(degree + 1) for upward in range(degree + 1 - across)
    ]
    lookup = {pair: number for number, pair in enumerate(node_pairs)}
    tables = []
    for rotations in range(3):
        new_order = []
        for node_pair in node_pairs:
            moved_pair = (node_pair[1], node_pair[0])
            for repeat in range(rotations):
                moved_pair = (moved_pair[1], degree - moved_pair[0] - moved_pair[1])
            new_order.append(lookup[moved_pair])
        tables.append(new_order)
    return np.array(tables, dtype=np.int32)


def round_up(value, step):
    return (value + step - 1) // step * step


def radices(count):
    out = []
    while count > 1:
        radix = max([r for r in range(2, 9) if count % r == 0], default=count)
        out.append(radix)
        count //= radix
    return out


def offset_of(position):
    return position - REACH if position < REACH else position - REACH + 1


def split(value):
    high = value.astype(BF16)
    low = (value - high.astype(F32)).astype(BF16)
    return high, low


def dot(a, b):
    return jnp.dot(a, b, preferred_element_type=F32)


def kernel(
    count,
    nq,
    nb,
    nf,
    *refs,
):
    whole = refs[:OPERANDS]
    out_ref = refs[OPERANDS]
    held = refs[OPERANDS + 1 : 2 * OPERANDS + 1]
    (
        q_ref,
        star_ref,
        minus_ref,
        plus_ref,
        limit_ref,
        deriv_ref,
        volume_ref,
        proj_ref,
        lift_ref,
        link_ref,
        orient_ref,
        send_ref,
        compact_ref,
        rotate_ref,
    ) = held
    (
        in_sem,
        a_der,
        a_vol,
        a_proj,
        a_lift,
        s_local,
        s_remote,
        t_send,
        series,
        b_mat,
        r_mat,
        vol,
        own,
        ic_two,
        io,
        faces,
        pool,
        picked,
        turned,
        across,
        b_lift,
        base,
        star_pair,
        min_out,
        min_in,
        send_buf,
        recv_buf,
        min_send_sem,
        min_recv_sem,
        send_sem,
        recv_sem,
    ) = refs[2 * OPERANDS + 1 :]
    elems = q_ref.shape[2]
    lanes = lax.broadcasted_iota(jnp.int32, (1, elems), 1)
    is_fine = lanes < FINE_DEV
    me = lax.axis_index("dom")
    bp = b_mat.shape[0] // 3
    rows_c = pool.shape[0] // 2
    half = rows_c // 2
    digits = radices(count)

    def fetch(number):
        return pltpu.make_async_copy(whole[number], held[number], in_sem.at[number])

    for number in (4, 5, 0, 1, 7, 11, 12, 9, 6, 2, 8, 10, 13, 3):
        fetch(number).start()

    def peer_of(number, step):
        stride = math.prod(digits[:number])
        radix = digits[number]
        digit = lax.rem(me // stride, radix)
        return me + (lax.rem(digit + step, radix) - digit) * stride

    barrier = pltpu.get_barrier_semaphore()
    expected = 0
    for number, radix in enumerate(digits):
        for step in range(1, radix):
            pl.semaphore_signal(
                barrier, inc=1, device_id=(peer_of(number, step),), device_id_type=MESH
            )
            expected += 1
    for position in range(2 * REACH):
        target = me - offset_of(position)

        @pl.when((target >= 0) & (target < count))
        def _():
            pl.semaphore_signal(barrier, inc=1, device_id=(target,), device_id_type=MESH)

    def min_copy(number, step):
        return pltpu.make_async_remote_copy(
            src_ref=min_out.at[number],
            dst_ref=min_in.at[number, step - 1],
            send_sem=min_send_sem.at[number, step - 1],
            recv_sem=min_recv_sem.at[number, step - 1],
            device_id=(peer_of(number, step),),
            device_id_type=MESH,
        )

    def min_start(number, value):
        min_out[number] = value
        for step in range(1, digits[number]):
            min_copy(number, step).start()

    def min_finish(number, value):
        for step in range(1, digits[number]):
            min_copy(number, step).wait_recv()
        for step in range(1, digits[number]):
            value = jnp.minimum(value, min_in[number, step - 1])
        return value

    def wide(x, width):
        high = x.astype(BF16).astype(F32)
        low = x - high
        if width > x.shape[1]:
            z = jnp.zeros((x.shape[0], width - x.shape[1]), F32)
            parts = [high, z, high, z, low, z]
        else:
            parts = [high, high, low]
        return jnp.concatenate(parts, axis=1)

    def square(target, source):
        for d in range(3):
            r_mat[d * nb : (d + 1) * nb, 0 : 3 * bp] = wide(source[d], bp)
        target[...] = r_mat[0 : 3 * nb, 0 : 3 * bp].astype(BF16)

    def make_proj():
        r_mat[0 : 4 * NODE_PAD, 0 : 3 * bp] = jnp.zeros((4 * NODE_PAD, 3 * bp), F32)
        for f in range(4):
            r_mat[f * NODE_PAD : f * NODE_PAD + nf, 0 : 3 * bp] = wide(proj_ref[:, f, :], bp)
        a_proj[...] = r_mat[0 : 4 * NODE_PAD, 0 : 3 * bp].astype(BF16)

    def make_lift():
        r_mat[0 : 4 * NODE_PAD, 0:128] = jnp.zeros((4 * NODE_PAD, 128), F32)
        for f in range(4):
            r_mat[f * NODE_PAD : f * NODE_PAD + nf, 0:nb] = lift_ref[:, f, :]
        turned_lift = jnp.transpose(r_mat[0 : 4 * NODE_PAD, 0:128])[0:nb]
        a_lift[...] = wide(turned_lift, 4 * NODE_PAD).astype(BF16)

    def fill(target_q, x):
        high, low = split(jnp.concatenate([x, jnp.zeros((bp - nb, elems), F32)], axis=0))
        b_mat[0:bp, target_q * elems : (target_q + 1) * elems] = high
        b_mat[bp : 2 * bp, target_q * elems : (target_q + 1) * elems] = low
        b_mat[2 * bp : 3 * bp, target_q * elems : (target_q + 1) * elems] = high

    def starred(a_ref, rows_ref, blocks, store):
        r_mat[:, 0 : blocks * elems] = dot(a_ref[...], b_mat[:, 0 : blocks * elems])

        def group(g, carry):
            sums = [None] * 3
            for d in range(3):
                for q in range(blocks):
                    block = r_mat[d * nb : (d + 1) * nb, q * elems : (q + 1) * elems]
                    for i in range(3):
                        row = rows_ref[g * 3 + i, q, d : d + 1, :]
                        term = row * block
                        sums[i] = term if sums[i] is None else sums[i] + term
            for i in range(3):
                store(g * 3 + i, sums[i])
            return carry

        lax.fori_loop(0, nq // 3, group, 0)

    def taylor(first, last):
        def step(k, carry):
            for q in range(nq):
                fill(q, series[k, q])

            def keep(p, value):
                series[k + 1, p] = -value

            starred(a_der, star_ref, nq, keep)
            return carry

        lax.fori_loop(first, last, step, 0)

    pairs = (nq + 1) // 2

    def taylor_fine():
        def step(k, carry):
            for j in range(pairs):
                fill(j, jnp.where(is_fine, series[k, 2 * j], series[k, min(2 * j + 1, nq - 1)]))

            def keep(p, value):
                series[k + 1, p] = -(value + pltpu.roll(value, FINE_DEV, 1))

            starred(a_der, star_pair, pairs, keep)
            return carry

        lax.fori_loop(0, ORDER - 1, step, 0)

    numbers = lax.broadcasted_iota(jnp.int32, (128, elems), 0)
    own_faces = s_local.shape[0]

    def make_sends():
        for g in range(REACH):
            sends = jnp.concatenate(
                [send_ref[2 * g : 2 * g + 1, :], send_ref[2 * g + 1 : 2 * g + 2, :]], axis=1
            )
            for v in range(0, own_faces, 128):
                t_send[v : v + 128, g * elems : (g + 1) * elems] = jnp.where(
                    numbers + v == sends, 1.0, 0.0
                ).astype(BF16)

    def make_local():
        for f in range(4):
            link = link_ref[f : f + 1, :]
            for v in range(0, own_faces, 128):
                s_local[v : v + 128, f * elems : (f + 1) * elems] = jnp.where(
                    numbers + v == link, 1.0, 0.0
                ).astype(BF16)

    def make_remote():
        for f in range(4):
            link = link_ref[f : f + 1, :]
            for g in range(REACH):
                spot = GROUP_SPOT[g] * 128
                s_remote[spot : spot + 128, f * elems : (f + 1) * elems] = jnp.where(
                    numbers + (g * 128 + own_faces) == link, 1.0, 0.0
                ).astype(BF16)
        for stage in range(2):
            for position in range(2 * REACH):
                source = me + offset_of(position)

                @pl.when((source < 0) | (source >= count))
                def _():
                    recv_buf[stage, position] = jnp.zeros(recv_buf.shape[2:], F32)

    def make_pairs():
        def one(p, carry):
            for j in range(pairs):
                first = star_ref[p, 2 * j][:, 0:FINE_DEV]
                if 2 * j + 1 < nq:
                    second = star_ref[p, 2 * j + 1][:, 0:FINE_DEV]
                else:
                    second = jnp.zeros_like(first)
                star_pair[p, j] = jnp.concatenate([first, second], axis=1)
            return carry

        lax.fori_loop(0, nq, one, 0)

    fetch(4).wait()
    least = jnp.where(is_fine, limit_ref[...], limit_ref[...] * 0.5)
    least = jnp.broadcast_to(jnp.min(least, axis=1, keepdims=True), (8, elems))
    fetch(5).wait()
    square(a_der, deriv_ref)
    fetch(0).wait()
    for q in range(nq):
        series[0, q] = q_ref[q]
    faces[...] = jnp.zeros(faces.shape, F32)
    below = jnp.minimum(me, REACH)
    above = jnp.minimum(count - 1 - me, REACH)
    pl.semaphore_wait(barrier, expected + below + above)
    if digits:
        min_start(0, least)
    fetch(1).wait()
    taylor(0, 2)
    if digits:
        least = min_finish(0, least)
        if len(digits) > 1:
            min_start(1, least)
    taylor(2, ORDER - 1)
    fetch(7).wait()
    make_proj()
    fetch(11).wait()
    make_sends()
    for number in range(1, len(digits)):
        least = min_finish(number, least)
        if number + 1 < len(digits):
            min_start(number + 1, least)
    step_fine = least[0:1, :]
    fetch(12).wait()

    weights = []
    weights_two = []
    power = step_fine
    for k in range(ORDER):
        weights.append(power * (1.0 / math.factorial(k + 1)))
        weights_two.append(weights[-1] * float(2 ** (k + 1) - 1))
        power = power * step_fine

    def block_copy(stage, position):
        return pltpu.make_async_remote_copy(
            src_ref=send_buf.at[stage, position],
            dst_ref=recv_buf.at[stage, position],
            send_sem=send_sem.at[stage, position],
            recv_sem=recv_sem.at[stage, position],
            device_id=(me - offset_of(position),),
            device_id_type=MESH,
        )

    def flux(solver_ref, data_ref, first):
        def face(f, carry):
            sums = [None] * nq
            for q in range(nq):
                block = data_ref[f, q * NODE_PAD : (q + 1) * NODE_PAD, :]
                for p in range(nq):
                    term = solver_ref[p, q, pl.ds(f, 1), :] * block
                    sums[p] = term if sums[p] is None else sums[p] + term
            spot = pl.ds(pl.multiple_of(f * NODE_PAD, 8), NODE_PAD)
            for p in range(nq):
                if first:
                    across[p, spot, :] = sums[p]
                else:
                    across[p, spot, :] = across[p, spot, :] + sums[p]
            return carry

        lax.fori_loop(0, 4, face, 0)

    def stage_work(stage):
        projected = dot(a_proj[...], b_mat[...])
        for f in range(4):
            for q in range(nq):
                faces[f, q * NODE_PAD : (q + 1) * NODE_PAD, :] = projected[
                    f * NODE_PAD : (f + 1) * NODE_PAD, q * elems : (q + 1) * elems
                ]
        for f in range(4):
            high, low = split(faces[f])
            pool[0:rows_c, f * elems : (f + 1) * elems] = dot(compact_ref[...], high).astype(BF16)
            pool[rows_c : 2 * rows_c, f * elems : (f + 1) * elems] = dot(
                compact_ref[...], low
            ).astype(BF16)
        for g in range(REACH):
            packed = dot(pool[...], t_send[:, g * elems : (g + 1) * elems])
            packed = packed[0:rows_c] + packed[rows_c : 2 * rows_c]
            upper, lower = packed[0:half], packed[half:rows_c]
            send_buf[stage, 2 * g] = jnp.where(is_fine, upper, pltpu.roll(lower, FINE_DEV, 1))
            send_buf[stage, 2 * g + 1] = jnp.where(is_fine, pltpu.roll(upper, FINE_DEV, 1), lower)
        for position in SEND_ORDER:
            target = me - offset_of(position)

            @pl.when((target >= 0) & (target < count))
            def _():
                block_copy(stage, position).start()

        if stage == 0:
            fetch(9).wait()
            make_local()
        picked[...] = dot(pool[...], s_local[...])
        if stage == 0:
            make_remote()
            own[...] = faces[...]
        else:
            for f in range(4):
                own[f] = jnp.where(is_fine, faces[f], faces[f] + own[f])
            for q in range(nq):
                fill(q, io[q])

        def keep(p, value):
            vol[p] = value

        if stage == 0:
            for number in (6, 2):
                fetch(number).wait()
            square(a_vol, volume_ref)
        starred(a_vol, star_ref, nq, keep)
        flux(minus_ref, own, True)
        if stage == 0:
            for number in (8, 10, 13, 3):
                fetch(number).wait()
            make_lift()
            make_pairs()

        def arrive(g):
            for position in (2 * g, 2 * g + 1):
                source = me + offset_of(position)

                @pl.when((source >= 0) & (source < count))
                def _():
                    block_copy(stage, position).wait_recv()

            first, second = recv_buf[stage, 2 * g], recv_buf[stage, 2 * g + 1]
            upper = jnp.where(is_fine, first, pltpu.roll(second, FINE_DEV, 1))
            lower = jnp.where(is_fine, pltpu.roll(first, FINE_DEV, 1), second)
            high, low = split(jnp.concatenate([upper, lower], axis=0))
            spot = GROUP_SPOT[g] * elems
            pool[0:rows_c, spot : spot + elems] = high
            pool[rows_c : 2 * rows_c, spot : spot + elems] = low

        remote = s_remote.shape[0]
        cut = remote - elems
        arrive(0)
        arrive(2)
        picked[...] = picked[...] + dot(pool[:, 0:cut], s_remote[0:cut, :])
        arrive(1)
        total = (picked[...] + dot(pool[:, cut:remote], s_remote[cut:remote, :])).astype(BF16)
        rows_n = rotate_ref.shape[0] // 3
        for f in range(4):
            three = dot(rotate_ref[...], total[:, f * elems : (f + 1) * elems])
            code = orient_ref[f : f + 1, :]
            new = jnp.where(
                code == 0,
                three[0:rows_n],
                jnp.where(code == 1, three[rows_n : 2 * rows_n], three[2 * rows_n :]),
            )
            if stage == 0:
                turned[f] = new
            else:
                turned[f] = jnp.where(is_fine, new, new + turned[f])
        flux(plus_ref, turned, False)
        for p in range(nq):
            high, low = split(across[p])
            rows = 4 * NODE_PAD
            b_lift[0:rows, p * elems : (p + 1) * elems] = high
            b_lift[rows : 2 * rows, p * elems : (p + 1) * elems] = low
            b_lift[2 * rows : 3 * rows, p * elems : (p + 1) * elems] = high
        return dot(a_lift[...], b_lift[...])

    def weighted(q, table):
        total = table[0] * series[0, q]
        for k in range(1, ORDER):
            total = total + table[k] * series[k, q]
        return total

    for q in range(nq):
        one = weighted(q, weights)
        two = weighted(q, weights_two)
        fill(q, one)
        ic_two[q] = two
        io[q] = one + two
    lifted = stage_work(0)
    for p in range(nq):
        mid = q_ref[p] + vol[p] - lifted[:, p * elems : (p + 1) * elems]
        base[p] = jnp.where(is_fine, mid, q_ref[p])
        series[0, p] = jnp.where(is_fine, mid, pltpu.roll(mid, FINE_DEV, 1))
    taylor_fine()
    for q in range(nq):
        one = weighted(q, weights)
        fill(q, jnp.where(is_fine, one, ic_two[q]))
        io[q] = jnp.where(is_fine, one, io[q])
    lifted = stage_work(1)
    for p in range(nq):
        out_ref[p] = base[p] + vol[p] - lifted[:, p * elems : (p + 1) * elems]

    for number, radix in enumerate(digits):
        for step in range(1, radix):
            min_copy(number, step).wait_send()
    for stage in range(2):
        for position in range(2 * REACH):
            target = me - offset_of(position)

            @pl.when((target >= 0) & (target < count))
            def _():
                block_copy(stage, position).wait_send()


def local(count, *args):
    q_state, face_proj, send_face = args[0], args[7], args[11]
    nq, nb, elems = q_state.shape
    nf = face_proj.shape[1]
    slots = send_face.shape[0] * send_face.shape[1]
    bp = round_up(nb, 16)
    rows_n = round_up(nq * NODE_PAD, 16)
    rows_c = round_up(nq * nf, 32)
    compact = np.zeros((rows_c, rows_n), np.float32)
    rotate = np.zeros((3 * rows_n, 2 * rows_c), np.float32)
    table = rotation_table(nf)
    for q in range(nq):
        for n in range(nf):
            compact[q * nf + n, q * NODE_PAD + n] = 1
            for h in range(3):
                rotate[h * rows_n + q * NODE_PAD + n, q * nf + table[h, n]] = 1
                rotate[h * rows_n + q * NODE_PAD + n, rows_c + q * nf + table[h, n]] = 1
    args = list(args)
    for number in (1, 2, 3):
        args[number] = jnp.transpose(args[number], (1, 2, 0, 3))
    args[4] = args[4].reshape(1, elems)
    args[7] = jnp.transpose(args[7], (1, 0, 2))
    args[8] = jnp.transpose(args[8], (2, 0, 1))
    args += [jnp.asarray(compact, BF16), jnp.asarray(rotate, BF16)]
    rounds = max(len(radices(count)), 1)
    widest = max([r - 1 for r in radices(count)] + [1])
    vm = pltpu.VMEM
    scratch = [vm(x.shape, x.dtype) for x in args] + [
        pltpu.SemaphoreType.DMA((OPERANDS,)),
        vm((3 * nb, 3 * bp), BF16),
        vm((3 * nb, 3 * bp), BF16),
        vm((4 * NODE_PAD, 3 * bp), BF16),
        vm((nb, 12 * NODE_PAD), BF16),
        vm((4 * elems, 4 * elems), BF16),
        vm((slots, 4 * elems), BF16),
        vm((4 * elems, slots), BF16),
        vm((ORDER, nq, nb, elems), F32),
        vm((3 * bp, nq * elems), BF16),
        vm((3 * nb, nq * elems), F32),
        vm((nq, nb, elems), F32),
        vm((4, rows_n, elems), F32),
        vm((nq, nb, elems), F32),
        vm((nq, nb, elems), F32),
        vm((4, rows_n, elems), F32),
        vm((2 * rows_c, 4 * elems), BF16),
        vm((2 * rows_c, 4 * elems), F32),
        vm((4, rows_n, elems), F32),
        vm((nq, 4 * NODE_PAD, elems), F32),
        vm((12 * NODE_PAD, nq * elems), BF16),
        vm((nq, nb, elems), F32),
        vm((nq, (nq + 1) // 2, 3, elems), F32),
        vm((rounds, 8, elems), F32),
        vm((rounds, widest, 8, elems), F32),
        vm((2, 2 * REACH, rows_c // 2, elems), F32),
        vm((2, 2 * REACH, rows_c // 2, elems), F32),
        pltpu.SemaphoreType.DMA((rounds, widest)),
        pltpu.SemaphoreType.DMA((rounds, widest)),
        pltpu.SemaphoreType.DMA((2, 2 * REACH)),
        pltpu.SemaphoreType.DMA((2, 2 * REACH)),
    ]
    return pl.pallas_call(
        functools.partial(kernel, count, nq, nb, nf),
        out_shape=jax.ShapeDtypeStruct(q_state.shape, F32),
        in_specs=[pl.BlockSpec(memory_space=pltpu.HBM)] * len(args),
        out_specs=pl.BlockSpec(memory_space=pltpu.VMEM),
        scratch_shapes=scratch,
        compiler_params=pltpu.CompilerParams(
            collective_id=0, has_side_effects=True, vmem_limit_bytes=62 * 1024 * 1024
        ),
    )(*args)


def solution(mesh):
    placed = (
        P(None, None, "dom"),
        P(None, None, None, "dom"),
        P(None, None, None, "dom"),
        P(None, None, None, "dom"),
        P("dom"),
        P(),
        P(),
        P(),
        P(),
        P(None, "dom"),
        P(None, "dom"),
        P(None, "dom"),
    )
    count = mesh.shape["dom"]
    return jax.shard_map(
        functools.partial(local, count),
        mesh=mesh,
        in_specs=placed,
        out_specs=P(None, None, "dom"),
        check_vma=False,
    )
```

```python
import functools
import math

import jax
import jax.numpy as jnp
import numpy as np
from jax import lax
from jax.experimental import pallas as pl
from jax.experimental.pallas import tpu as pltpu
from jax.sharding import PartitionSpec as P

ORDER = 6
REACH = 3
FINE_DEV = 64
NODE_PAD = 24
F32 = jnp.float32
BF16 = jnp.bfloat16
MESH = pl.DeviceIdType.MESH
OPERANDS = 14
SEND_ORDER = (0, 5, 1, 4, 2, 3)
GROUP_SPOT = (0, 2, 1)


def rotation_table(node_count):
    degree = 0
    while (degree + 1) * (degree + 2) // 2 < node_count:
        degree += 1
    node_pairs = [
        (across, upward) for across in range(degree + 1) for upward in range(degree + 1 - across)
    ]
    lookup = {pair: number for number, pair in enumerate(node_pairs)}
    tables = []
    for rotations in range(3):
        new_order = []
        for node_pair in node_pairs:
            moved_pair = (node_pair[1], node_pair[0])
            for repeat in range(rotations):
                moved_pair = (moved_pair[1], degree - moved_pair[0] - moved_pair[1])
            new_order.append(lookup[moved_pair])
        tables.append(new_order)
    return np.array(tables, dtype=np.int32)


def round_up(value, step):
    return (value + step - 1) // step * step


def radices(count):
    out = []
    while count > 1:
        radix = max([r for r in range(2, 9) if count % r == 0], default=count)
        out.append(radix)
        count //= radix
    return out


def offset_of(position):
    return position - REACH if position < REACH else position - REACH + 1


def split(value):
    high = value.astype(BF16)
    low = (value - high.astype(F32)).astype(BF16)
    return high, low


def dot(a, b):
    return jnp.dot(a, b, preferred_element_type=F32)


def kernel(
    count,
    nq,
    nb,
    nf,
    *refs,
):
    whole = refs[:OPERANDS]
    out_ref = refs[OPERANDS]
    held = refs[OPERANDS + 1 : 2 * OPERANDS + 1]
    (
        q_ref,
        star_ref,
        minus_ref,
        plus_ref,
        limit_ref,
        deriv_ref,
        volume_ref,
        proj_ref,
        lift_ref,
        link_ref,
        orient_ref,
        send_ref,
        compact_ref,
        rotate_ref,
    ) = held
    (
        in_sem,
        a_der,
        a_vol,
        a_proj,
        a_lift,
        s_local,
        s_remote,
        t_send,
        series,
        b_mat,
        r_mat,
        vol,
        own,
        ic_two,
        io,
        faces,
        pool,
        picked,
        turned,
        across,
        b_lift,
        base,
        star_pair,
        min_out,
        min_in,
        send_buf,
        recv_buf,
        min_send_sem,
        min_recv_sem,
        send_sem,
        recv_sem,
    ) = refs[2 * OPERANDS + 1 :]
    elems = q_ref.shape[2]
    lanes = lax.broadcasted_iota(jnp.int32, (1, elems), 1)
    is_fine = lanes < FINE_DEV
    me = lax.axis_index("dom")
    bp = b_mat.shape[0] // 3
    rows_c = pool.shape[0] // 2
    half = rows_c // 2
    digits = radices(count)

    def fetch(number):
        return pltpu.make_async_copy(whole[number], held[number], in_sem.at[number])

    for number in (4, 5, 0, 1, 7, 11, 12, 9, 6, 2, 8, 10, 13, 3):
        fetch(number).start()

    def peer_of(number, step):
        stride = math.prod(digits[:number])
        radix = digits[number]
        digit = lax.rem(me // stride, radix)
        return me + (lax.rem(digit + step, radix) - digit) * stride

    barrier = pltpu.get_barrier_semaphore()
    expected = 0
    for number, radix in enumerate(digits):
        for step in range(1, radix):
            pl.semaphore_signal(
                barrier, inc=1, device_id=(peer_of(number, step),), device_id_type=MESH
            )
            expected += 1
    for position in range(2 * REACH):
        target = me - offset_of(position)

        @pl.when((target >= 0) & (target < count))
        def _():
            pl.semaphore_signal(barrier, inc=1, device_id=(target,), device_id_type=MESH)

    def min_copy(number, step):
        return pltpu.make_async_remote_copy(
            src_ref=min_out.at[number],
            dst_ref=min_in.at[number, step - 1],
            send_sem=min_send_sem.at[number, step - 1],
            recv_sem=min_recv_sem.at[number, step - 1],
            device_id=(peer_of(number, step),),
            device_id_type=MESH,
        )

    def min_start(number, value):
        min_out[number] = value
        for step in range(1, digits[number]):
            min_copy(number, step).start()

    def min_finish(number, value):
        for step in range(1, digits[number]):
            min_copy(number, step).wait_recv()
        for step in range(1, digits[number]):
            value = jnp.minimum(value, min_in[number, step - 1])
        return value

    def wide(x, width):
        high = x.astype(BF16).astype(F32)
        low = x - high
        if width > x.shape[1]:
            z = jnp.zeros((x.shape[0], width - x.shape[1]), F32)
            parts = [high, z, high, z, low, z]
        else:
            parts = [high, high, low]
        return jnp.concatenate(parts, axis=1)

    def square(target, source):
        for d in range(3):
            r_mat[d * nb : (d + 1) * nb, 0 : 3 * bp] = wide(source[d], bp)
        target[...] = r_mat[0 : 3 * nb, 0 : 3 * bp].astype(BF16)

    def make_proj():
        r_mat[0 : 4 * NODE_PAD, 0 : 3 * bp] = jnp.zeros((4 * NODE_PAD, 3 * bp), F32)
        for f in range(4):
            r_mat[f * NODE_PAD : f * NODE_PAD + nf, 0 : 3 * bp] = wide(proj_ref[:, f, :], bp)
        a_proj[...] = r_mat[0 : 4 * NODE_PAD, 0 : 3 * bp].astype(BF16)

    def make_lift():
        r_mat[0 : 4 * NODE_PAD, 0:128] = jnp.zeros((4 * NODE_PAD, 128), F32)
        for f in range(4):
            r_mat[f * NODE_PAD : f * NODE_PAD + nf, 0:nb] = lift_ref[:, f, :]
        turned_lift = jnp.transpose(r_mat[0 : 4 * NODE_PAD, 0:128])[0:nb]
        a_lift[...] = wide(turned_lift, 4 * NODE_PAD).astype(BF16)

    def fill(target_q, x):
        high, low = split(jnp.concatenate([x, jnp.zeros((bp - nb, elems), F32)], axis=0))
        b_mat[0:bp, target_q * elems : (target_q + 1) * elems] = high
        b_mat[bp : 2 * bp, target_q * elems : (target_q + 1) * elems] = low
        b_mat[2 * bp : 3 * bp, target_q * elems : (target_q + 1) * elems] = high

    def starred(a_ref, rows_ref, blocks, store):
        r_mat[:, 0 : blocks * elems] = dot(a_ref[...], b_mat[:, 0 : blocks * elems])

        def group(g, carry):
            sums = [None] * 3
            for d in range(3):
                for q in range(blocks):
                    block = r_mat[d * nb : (d + 1) * nb, q * elems : (q + 1) * elems]
                    for i in range(3):
                        row = rows_ref[g * 3 + i, q, d : d + 1, :]
                        term = row * block
                        sums[i] = term if sums[i] is None else sums[i] + term
            for i in range(3):
                store(g * 3 + i, sums[i])
            return carry

        lax.fori_loop(0, nq // 3, group, 0, unroll=True)

    def taylor(first, last):
        def step(k, carry):
            for q in range(nq):
                fill(q, series[k, q])

            def keep(p, value):
                series[k + 1, p] = -value

            starred(a_der, star_ref, nq, keep)
            return carry

        lax.fori_loop(first, last, step, 0)

    pairs = (nq + 1) // 2

    def taylor_fine():
        def step(k, carry):
            for j in range(pairs):
                fill(j, jnp.where(is_fine, series[k, 2 * j], series[k, min(2 * j + 1, nq - 1)]))

            def keep(p, value):
                series[k + 1, p] = -(value + pltpu.roll(value, FINE_DEV, 1))

            starred(a_der, star_pair, pairs, keep)
            return carry

        lax.fori_loop(0, ORDER - 1, step, 0)

    numbers = lax.broadcasted_iota(jnp.int32, (128, elems), 0)
    own_faces = s_local.shape[0]

    def make_sends():
        for g in range(REACH):
            sends = jnp.concatenate(
                [send_ref[2 * g : 2 * g + 1, :], send_ref[2 * g + 1 : 2 * g + 2, :]], axis=1
            )
            for v in range(0, own_faces, 128):
                t_send[v : v + 128, g * elems : (g + 1) * elems] = jnp.where(
                    numbers + v == sends, 1.0, 0.0
                ).astype(BF16)

    def make_local():
        for f in range(4):
            link = link_ref[f : f + 1, :]
            for v in range(0, own_faces, 128):
                s_local[v : v + 128, f * elems : (f + 1) * elems] = jnp.where(
                    numbers + v == link, 1.0, 0.0
                ).astype(BF16)

    def make_remote():
        for f in range(4):
            link = link_ref[f : f + 1, :]
            for g in range(REACH):
                spot = GROUP_SPOT[g] * 128
                s_remote[spot : spot + 128, f * elems : (f + 1) * elems] = jnp.where(
                    numbers + (g * 128 + own_faces) == link, 1.0, 0.0
                ).astype(BF16)
        for stage in range(2):
            for position in range(2 * REACH):
                source = me + offset_of(position)

                @pl.when((source < 0) | (source >= count))
                def _():
                    recv_buf[stage, position] = jnp.zeros(recv_buf.shape[2:], F32)

    def make_pairs():
        def one(p, carry):
            for j in range(pairs):
                first = star_ref[p, 2 * j][:, 0:FINE_DEV]
                if 2 * j + 1 < nq:
                    second = star_ref[p, 2 * j + 1][:, 0:FINE_DEV]
                else:
                    second = jnp.zeros_like(first)
                star_pair[p, j] = jnp.concatenate([first, second], axis=1)
            return carry

        lax.fori_loop(0, nq, one, 0)

    fetch(4).wait()
    least = jnp.where(is_fine, limit_ref[...], limit_ref[...] * 0.5)
    least = jnp.broadcast_to(jnp.min(least, axis=1, keepdims=True), (8, elems))
    fetch(5).wait()
    square(a_der, deriv_ref)
    fetch(0).wait()
    for q in range(nq):
        series[0, q] = q_ref[q]
    faces[...] = jnp.zeros(faces.shape, F32)
    below = jnp.minimum(me, REACH)
    above = jnp.minimum(count - 1 - me, REACH)
    pl.semaphore_wait(barrier, expected + below + above)
    if digits:
        min_start(0, least)
    fetch(1).wait()
    taylor(0, 2)
    if digits:
        least = min_finish(0, least)
        if len(digits) > 1:
            min_start(1, least)
    taylor(2, ORDER - 1)
    fetch(7).wait()
    make_proj()
    fetch(11).wait()
    make_sends()
    for number in range(1, len(digits)):
        least = min_finish(number, least)
        if number + 1 < len(digits):
            min_start(number + 1, least)
    step_fine = least[0:1, :]
    fetch(12).wait()

    weights = []
    weights_two = []
    power = step_fine
    for k in range(ORDER):
        weights.append(power * (1.0 / math.factorial(k + 1)))
        weights_two.append(weights[-1] * float(2 ** (k + 1) - 1))
        power = power * step_fine

    def block_copy(stage, position):
        return pltpu.make_async_remote_copy(
            src_ref=send_buf.at[stage, position],
            dst_ref=recv_buf.at[stage, position],
            send_sem=send_sem.at[stage, position],
            recv_sem=recv_sem.at[stage, position],
            device_id=(me - offset_of(position),),
            device_id_type=MESH,
        )

    def flux(solver_ref, data_ref, first):
        def face(f, carry):
            sums = [None] * nq
            for q in range(nq):
                block = data_ref[f, q * NODE_PAD : (q + 1) * NODE_PAD, :]
                for p in range(nq):
                    term = solver_ref[p, q, pl.ds(f, 1), :] * block
                    sums[p] = term if sums[p] is None else sums[p] + term
            spot = pl.ds(pl.multiple_of(f * NODE_PAD, 8), NODE_PAD)
            for p in range(nq):
                if first:
                    across[p, spot, :] = sums[p]
                else:
                    across[p, spot, :] = across[p, spot, :] + sums[p]
            return carry

        lax.fori_loop(0, 4, face, 0, unroll=True)

    def stage_work(stage):
        projected = dot(a_proj[...], b_mat[...])
        for f in range(4):
            for q in range(nq):
                faces[f, q * NODE_PAD : (q + 1) * NODE_PAD, :] = projected[
                    f * NODE_PAD : (f + 1) * NODE_PAD, q * elems : (q + 1) * elems
                ]
        for f in range(4):
            high, low = split(faces[f])
            pool[0:rows_c, f * elems : (f + 1) * elems] = dot(compact_ref[...], high).astype(BF16)
            pool[rows_c : 2 * rows_c, f * elems : (f + 1) * elems] = dot(
                compact_ref[...], low
            ).astype(BF16)
        for g in range(REACH):
            packed = dot(pool[...], t_send[:, g * elems : (g + 1) * elems])
            packed = packed[0:rows_c] + packed[rows_c : 2 * rows_c]
            upper, lower = packed[0:half], packed[half:rows_c]
            send_buf[stage, 2 * g] = jnp.where(is_fine, upper, pltpu.roll(lower, FINE_DEV, 1))
            send_buf[stage, 2 * g + 1] = jnp.where(is_fine, pltpu.roll(upper, FINE_DEV, 1), lower)
        for position in SEND_ORDER:
            target = me - offset_of(position)

            @pl.when((target >= 0) & (target < count))
            def _():
                block_copy(stage, position).start()

        if stage == 0:
            fetch(9).wait()
            make_local()
        picked[...] = dot(pool[...], s_local[...])
        if stage == 0:
            make_remote()
            own[...] = faces[...]
        else:
            for f in range(4):
                own[f] = jnp.where(is_fine, faces[f], faces[f] + own[f])
            for q in range(nq):
                fill(q, io[q])

        def keep(p, value):
            vol[p] = value

        if stage == 0:
            for number in (6, 2):
                fetch(number).wait()
            square(a_vol, volume_ref)
        starred(a_vol, star_ref, nq, keep)
        flux(minus_ref, own, True)
        if stage == 0:
            for number in (8, 10, 13, 3):
                fetch(number).wait()
            make_lift()
            make_pairs()

        def arrive(g):
            for position in (2 * g, 2 * g + 1):
                source = me + offset_of(position)

                @pl.when((source >= 0) & (source < count))
                def _():
                    block_copy(stage, position).wait_recv()

            first, second = recv_buf[stage, 2 * g], recv_buf[stage, 2 * g + 1]
            upper = jnp.where(is_fine, first, pltpu.roll(second, FINE_DEV, 1))
            lower = jnp.where(is_fine, pltpu.roll(first, FINE_DEV, 1), second)
            high, low = split(jnp.concatenate([upper, lower], axis=0))
            spot = GROUP_SPOT[g] * elems
            pool[0:rows_c, spot : spot + elems] = high
            pool[rows_c : 2 * rows_c, spot : spot + elems] = low

        remote = s_remote.shape[0]
        cut = remote - elems
        arrive(0)
        arrive(2)
        picked[...] = picked[...] + dot(pool[:, 0:cut], s_remote[0:cut, :])
        arrive(1)
        total = (picked[...] + dot(pool[:, cut:remote], s_remote[cut:remote, :])).astype(BF16)
        rows_n = rotate_ref.shape[0] // 3
        for f in range(4):
            three = dot(rotate_ref[...], total[:, f * elems : (f + 1) * elems])
            code = orient_ref[f : f + 1, :]
            new = jnp.where(
                code == 0,
                three[0:rows_n],
                jnp.where(code == 1, three[rows_n : 2 * rows_n], three[2 * rows_n :]),
            )
            if stage == 0:
                turned[f] = new
            else:
                turned[f] = jnp.where(is_fine, new, new + turned[f])
        flux(plus_ref, turned, False)
        for p in range(nq):
            high, low = split(across[p])
            rows = 4 * NODE_PAD
            b_lift[0:rows, p * elems : (p + 1) * elems] = high
            b_lift[rows : 2 * rows, p * elems : (p + 1) * elems] = low
            b_lift[2 * rows : 3 * rows, p * elems : (p + 1) * elems] = high
        return dot(a_lift[...], b_lift[...])

    def weighted(q, table):
        total = table[0] * series[0, q]
        for k in range(1, ORDER):
            total = total + table[k] * series[k, q]
        return total

    for q in range(nq):
        one = weighted(q, weights)
        two = weighted(q, weights_two)
        fill(q, one)
        ic_two[q] = two
        io[q] = one + two
    lifted = stage_work(0)
    for p in range(nq):
        mid = q_ref[p] + vol[p] - lifted[:, p * elems : (p + 1) * elems]
        base[p] = jnp.where(is_fine, mid, q_ref[p])
        series[0, p] = jnp.where(is_fine, mid, pltpu.roll(mid, FINE_DEV, 1))
    taylor_fine()
    for q in range(nq):
        one = weighted(q, weights)
        fill(q, jnp.where(is_fine, one, ic_two[q]))
        io[q] = jnp.where(is_fine, one, io[q])
    lifted = stage_work(1)
    for p in range(nq):
        out_ref[p] = base[p] + vol[p] - lifted[:, p * elems : (p + 1) * elems]

    for number, radix in enumerate(digits):
        for step in range(1, radix):
            min_copy(number, step).wait_send()
    for stage in range(2):
        for position in range(2 * REACH):
            target = me - offset_of(position)

            @pl.when((target >= 0) & (target < count))
            def _():
                block_copy(stage, position).wait_send()


def local(count, *args):
    q_state, face_proj, send_face = args[0], args[7], args[11]
    nq, nb, elems = q_state.shape
    nf = face_proj.shape[1]
    slots = send_face.shape[0] * send_face.shape[1]
    bp = round_up(nb, 16)
    rows_n = round_up(nq * NODE_PAD, 16)
    rows_c = round_up(nq * nf, 32)
    compact = np.zeros((rows_c, rows_n), np.float32)
    rotate = np.zeros((3 * rows_n, 2 * rows_c), np.float32)
    table = rotation_table(nf)
    for q in range(nq):
        for n in range(nf):
            compact[q * nf + n, q * NODE_PAD + n] = 1
            for h in range(3):
                rotate[h * rows_n + q * NODE_PAD + n, q * nf + table[h, n]] = 1
                rotate[h * rows_n + q * NODE_PAD + n, rows_c + q * nf + table[h, n]] = 1
    args = list(args)
    for number in (1, 2, 3):
        args[number] = jnp.transpose(args[number], (1, 2, 0, 3))
    args[4] = args[4].reshape(1, elems)
    args[7] = jnp.transpose(args[7], (1, 0, 2))
    args[8] = jnp.transpose(args[8], (2, 0, 1))
    args += [jnp.asarray(compact, BF16), jnp.asarray(rotate, BF16)]
    rounds = max(len(radices(count)), 1)
    widest = max([r - 1 for r in radices(count)] + [1])
    vm = pltpu.VMEM
    scratch = [vm(x.shape, x.dtype) for x in args] + [
        pltpu.SemaphoreType.DMA((OPERANDS,)),
        vm((3 * nb, 3 * bp), BF16),
        vm((3 * nb, 3 * bp), BF16),
        vm((4 * NODE_PAD, 3 * bp), BF16),
        vm((nb, 12 * NODE_PAD), BF16),
        vm((4 * elems, 4 * elems), BF16),
        vm((slots, 4 * elems), BF16),
        vm((4 * elems, slots), BF16),
        vm((ORDER, nq, nb, elems), F32),
        vm((3 * bp, nq * elems), BF16),
        vm((3 * nb, nq * elems), F32),
        vm((nq, nb, elems), F32),
        vm((4, rows_n, elems), F32),
        vm((nq, nb, elems), F32),
        vm((nq, nb, elems), F32),
        vm((4, rows_n, elems), F32),
        vm((2 * rows_c, 4 * elems), BF16),
        vm((2 * rows_c, 4 * elems), F32),
        vm((4, rows_n, elems), F32),
        vm((nq, 4 * NODE_PAD, elems), F32),
        vm((12 * NODE_PAD, nq * elems), BF16),
        vm((nq, nb, elems), F32),
        vm((nq, (nq + 1) // 2, 3, elems), F32),
        vm((rounds, 8, elems), F32),
        vm((rounds, widest, 8, elems), F32),
        vm((2, 2 * REACH, rows_c // 2, elems), F32),
        vm((2, 2 * REACH, rows_c // 2, elems), F32),
        pltpu.SemaphoreType.DMA((rounds, widest)),
        pltpu.SemaphoreType.DMA((rounds, widest)),
        pltpu.SemaphoreType.DMA((2, 2 * REACH)),
        pltpu.SemaphoreType.DMA((2, 2 * REACH)),
    ]
    return pl.pallas_call(
        functools.partial(kernel, count, nq, nb, nf),
        out_shape=jax.ShapeDtypeStruct(q_state.shape, F32),
        in_specs=[pl.BlockSpec(memory_space=pltpu.HBM)] * len(args),
        out_specs=pl.BlockSpec(memory_space=pltpu.VMEM),
        scratch_shapes=scratch,
        compiler_params=pltpu.CompilerParams(
            collective_id=0, has_side_effects=True, vmem_limit_bytes=62 * 1024 * 1024
        ),
    )(*args)


def solution(mesh):
    placed = (
        P(None, None, "dom"),
        P(None, None, None, "dom"),
        P(None, None, None, "dom"),
        P(None, None, None, "dom"),
        P("dom"),
        P(),
        P(),
        P(),
        P(),
        P(None, "dom"),
        P(None, "dom"),
        P(None, "dom"),
    )
    count = mesh.shape["dom"]
    return jax.shard_map(
        functools.partial(local, count),
        mesh=mesh,
        in_specs=placed,
        out_specs=P(None, None, "dom"),
        check_vma=False,
    )
```
